512 devices in a mesh: leaf: 64 (over y, x, z_lo), row: 8 (over z_hi, core).
Axes of the slice: x: 4, y: 8, z: 8 (z_hi: 4, z_lo: 2; z = z_hi * 2 + z_lo), core: 2. Of those that a mesh axis runs over, the one named last changes fastest.
Arguments:
- coupling: bfloat16 [64, 4096, 4096], P('leaf', 'row'), may hold values from -0.0390625 to 0.0390625
- rhs: bfloat16 [64, 4096, 128], P('leaf', 'row'), may hold values from -6 to 6
- left_factors: bfloat16 [64, 4096, 384], P('leaf', 'row'), may hold values from -6 to 6
- right_factors: bfloat16 [64, 4096, 384], P('leaf', 'row'), may hold values from -0.0014648438 to 0.0014648438
Outputs:
- solution: bfloat16 [64, 4096, 128], P('leaf', 'row')
The draws below stay inside these ranges and needn't reach their ends.
All inputs are finite; a program needn't handle non-finite values.
Results may differ from the reference program's by a relative error of at most 0.001.
Values may be sent and summed in bfloat16 or wider, within the bound.
No kernel may reach another device: no remote copies, remote signals or barrier semaphores. Data moves between devices by JAX's collectives and lax.ppermute only.
A program may use at most 64 MiB of HBM per device.

```python
import jax
import jax.numpy as jnp
from jax import lax

M = 4096
R = 128
B = 128
LEVELS = 3
LEAVES = 64


def block_levels(rng, extent, split, least, high):
    factor_of, own = 1.0, jax.random.fold_in(rng, 6)
    for position, shards_of in split:
        steps = jnp.exp(jax.random.uniform(jax.random.fold_in(own, position), (shards_of,), jnp.float32, least / len(split), high / len(split)))
        factor_of = factor_of * jnp.repeat(steps, extent[position] // shards_of).reshape([-1 if axis == position else 1 for axis in range(len(extent))])
    return factor_of


def normal_values(own_key, shape, deviation, most, cuts=(), kind=jnp.bfloat16):
    entries = jax.random.normal(own_key, shape, jnp.float32) * deviation
    if len(cuts) > 0:
        entries = block_levels(own_key, shape, cuts, -0.22, 0.18) * entries
    return jnp.clip(entries, min=-most, max=most).astype(kind)


def setup_inputs(seed: int = 0) -> dict:
    key_list = jax.random.split(jax.random.key(seed), 5)
    return {
        "coupling": normal_values(key_list[0], (LEAVES, M, M), (6 * M) ** -0.5, 0.0390625, ((0, 64), (1, 8))),
        "rhs": normal_values(key_list[1], (LEAVES, M, B), 1.0, 6.0, ((0, 64), (1, 8))),
        "left_factors": normal_values(key_list[2], (LEAVES, M, LEVELS * R), 1.0, 6.0, ((0, 64), (1, 8))),
        "right_factors": normal_values(key_list[3], (LEAVES, M, LEVELS * R), (32 * M * R) ** -0.5, 0.0014648438, ((0, 64), (1, 8))),
    }


def apply_leaf(pair):
    block, columns = pair
    return columns.astype(jnp.float32) + jnp.dot(block.astype(jnp.float32), columns.astype(jnp.float32), preferred_element_type=jnp.float32)

def reference(coupling, rhs, left_factors, right_factors):
    columns = jnp.concatenate([rhs, left_factors], axis=2)
    remaining_blocks = lax.map(apply_leaf, (coupling, columns))
    leaves = remaining_blocks.shape[0]
    highest_precision = lax.Precision.HIGHEST
    identity = jnp.eye(R, dtype=jnp.float32)
    for level in range(LEVELS):
        leading_block = remaining_blocks[:, :, B:B + R]
        other_blocks = jnp.concatenate([remaining_blocks[:, :, :B], remaining_blocks[:, :, B + R:]], axis=2)
        cholesky_factor = right_factors[:, :, level * R:(level + 1) * R].astype(jnp.float32)
        joined_pieces = jnp.concatenate([leading_block, other_blocks], axis=2)
        partial_value_sum = jnp.einsum('fxh,fxv->fhv', cholesky_factor, joined_pieces, precision=highest_precision)
        span = 2 ** level
        nodes = partial_value_sum.reshape(leaves // (2 * span), 2, span, R, -1).sum(axis=2)
        other = nodes[:, ::-1]
        e_own = nodes[..., :R]
        f_own = nodes[..., R:]
        e_other = other[..., :R]
        f_other = other[..., R:]
        system = identity - jnp.einsum('gsij,gsjk->gsik', e_other, e_own, precision=highest_precision)
        right = f_other - jnp.einsum('gsij,gsjk->gsik', e_other, f_own, precision=highest_precision)
        coef = jnp.linalg.solve(system, right)
        leaf_coefficients = jnp.broadcast_to(coef[:, :, None], (leaves // (2 * span), 2, span) + coef.shape[2:])
        leaf_coefficients = leaf_coefficients.reshape((leaves,) + coef.shape[2:])
        remaining_blocks = other_blocks - jnp.einsum('dke,deo->dko', leading_block, leaf_coefficients, precision=highest_precision)
    return remaining_blocks.astype(jnp.bfloat16)
```

```python
import jax
import jax.numpy as jnp
from jax import lax
from jax.experimental import pallas as pl
from jax.experimental.pallas import tpu as pltpu
from jax.sharding import PartitionSpec as P

R = 128
F32 = jnp.float32
BF16 = jnp.bfloat16
VMEM_BYTES = 48 * 1024 * 1024


def dot(a, b):
    return jnp.dot(a, b, precision=lax.Precision.HIGHEST, preferred_element_type=F32)


def solve(s, right, c_ref, p_ref):
    c = right + dot(s, right)
    p = dot(s, s)
    for _ in range(2):
        c = c + dot(p, c)
        p = dot(p, p)
    c_ref[...] = c
    p_ref[...] = p
    left = jnp.sum(p * p)
    good = jnp.logical_and(left < 0.25, jnp.sum(s * s) < 64.0)

    @pl.when(good)
    def _():
        def more(_):
            q = p_ref[...]
            c_ref[...] = c_ref[...] + dot(q, c_ref[...])
            q = dot(q, q)
            p_ref[...] = q
            return jnp.sum(q * q)

        lax.while_loop(lambda size: size > 1e-15, more, left)

    @pl.when(jnp.logical_not(good))
    def _():
        eye = (lax.broadcasted_iota(jnp.int32, (R, R), 0) == lax.broadcasted_iota(jnp.int32, (R, R), 1)).astype(F32)
        a = eye - s
        one = jnp.max(jnp.sum(jnp.abs(a), axis=0))
        most = jnp.max(jnp.sum(jnp.abs(a), axis=1))
        p_ref[...] = (a / one).T / most

        def again(state):
            step, old, new = state
            still = jnp.logical_or(new > 0.01, new < 0.25 * old)
            return jnp.logical_and(step < 200, jnp.logical_and(new > 1e-12, still))

        def newton(state):
            x = p_ref[...]
            res = eye - dot(a, x)
            p_ref[...] = x + dot(x, res)
            return (state[0] + 1, state[2], jnp.sum(res * res))

        lax.while_loop(again, newton, (jnp.int32(0), jnp.float32(1e30), jnp.float32(1e29)))
        x = p_ref[...]
        c_ref[...] = dot(x, right)
        for _ in range(2):
            c_ref[...] = c_ref[...] + dot(x, right - dot(a, c_ref[...]))


def apply_kernel(where_ref, block_ref, cols_ref, own_ref, v_ref, y_ref, keep_ref, send_ref, gram_ref):
    k = pl.program_id(0)

    @pl.when(k == 0)
    def _():
        y_ref[...] = own_ref[...].astype(F32)

    y_ref[...] += jnp.dot(block_ref[...], cols_ref[...], preferred_element_type=F32)

    @pl.when(k == pl.num_programs(0) - 1)
    def _():
        core = where_ref[0]
        rest = y_ref[...]
        total = None
        for _ in range(3):
            piece = rest.astype(BF16)
            rest = rest - piece.astype(F32)
            term = lax.dot_general(v_ref[...], piece, (((0,), (0,)), ((), ())), preferred_element_type=F32)
            total = term if total is None else total + term
        gram_ref[...] = total.reshape(gram_ref.shape)
        keep_ref[...] = gram_ref[core]
        send_ref[...] = gram_ref[1 - core]


def apply_leaf(where, block, gathered, own, v):
    m, width = own.shape
    steps = block.shape[1] // m
    half = v.shape[1] // 2
    return pl.pallas_call(
        apply_kernel,
        grid_spec=pltpu.PrefetchScalarGridSpec(
            num_scalar_prefetch=1,
            grid=(steps,),
            in_specs=[
                pl.BlockSpec((m, m), lambda k, w: (0, k)),
                pl.BlockSpec((m, width), lambda k, w: (k, 0)),
                pl.BlockSpec((m, width), lambda k, w: (0, 0)),
                pl.BlockSpec(v.shape, lambda k, w: (0, 0)),
            ],
            out_specs=[
                pl.BlockSpec((m, width), lambda k, w: (0, 0)),
                pl.BlockSpec((half, width), lambda k, w: (0, 0)),
                pl.BlockSpec((half, width), lambda k, w: (0, 0)),
            ],
            scratch_shapes=[pltpu.VMEM((2, half, width), F32)],
        ),
        out_shape=[
            jax.ShapeDtypeStruct((m, width), F32),
            jax.ShapeDtypeStruct((half, width), F32),
            jax.ShapeDtypeStruct((half, width), F32),
        ],
        compiler_params=pltpu.CompilerParams(vmem_limit_bytes=VMEM_BYTES),
    )(where, block, gathered, own, v)


def first_level(where_ref, own_ref, other_ref, coef_ref, half_ref, full_ref, p_ref):
    core, leaf = where_ref[0], where_ref[1]
    full_ref[core] = own_ref[...]
    full_ref[1 - core] = other_ref[...]
    a, b = leaf, 1 - leaf
    lead = full_ref[0, a, :R, :]
    product = dot(full_ref[0, b, :R, :R], lead)
    right = full_ref[0, b, :R, R:] - product[:, R:]
    solve(product[:, :R], right, coef_ref, p_ref)
    coef = coef_ref[...]
    coef_b = lead[:, R:] - dot(lead[:, :R], coef)

    def update(node, c):
        rows = full_ref[core, node, 64:, :] if False else None
        return rows

    @pl.when(core == 0)
    def _():
        total = None
        for node, c in ((a, coef), (b, coef_b)):
            rows = jnp.concatenate([full_ref[0, node, R:, :], full_ref[1, node, :64, :]], axis=0)
            term = rows[:, R:] - dot(rows[:, :R], c)
            total = term if total is None else total + term
        half_ref[...] = total

    @pl.when(core == 1)
    def _():
        total = None
        for node, c in ((a, coef), (b, coef_b)):
            rows = full_ref[1, node, 64:, :]
            term = rows[:, R:] - dot(rows[:, :R], c)
            total = term if total is None else total + term
        half_ref[...] = total


def last_levels(where_ref, own_ref, other_ref, coef_ref, y_ref, out_ref, full_ref, c_ref, d_ref, p_ref):
    core, node = where_ref[0], where_ref[2]
    full_ref[core] = own_ref[...]
    full_ref[1 - core] = other_ref[...]

    sums = []
    for index, (a, b) in enumerate(((node, node ^ 1), (node ^ 2, node ^ 3))):
        lead = full_ref[0, a]
        product = dot(full_ref[0, b, :, :R], lead)
        right = full_ref[0, b, :, R:] - product[:, R:]
        solve(product[:, :R], right, c_ref.at[index], p_ref)
        coef_a = c_ref[index]
        coef_b = lead[:, R:] - dot(lead[:, :R], coef_a)
        total = None
        for place, c in ((a, coef_a), (b, coef_b)):
            rows = full_ref[1, place]
            term = rows[:, R:] - dot(rows[:, :R], c)
            total = term if total is None else total + term
        sums.append(total)
    own, other = sums
    product = dot(other[:, :R], own)
    solve(product[:, :R], other[:, R:] - product[:, R:], d_ref, p_ref)
    x2 = d_ref[...]
    c1 = c_ref[0]
    c0 = coef_ref[...]
    x1 = c1[:, R:] - dot(c1[:, :R], x2)
    x0 = c0[:, 2 * R :] - dot(c0[:, :R], x1) - dot(c0[:, R : 2 * R], x2)
    x = jnp.concatenate([x0, x1, x2], axis=0)
    out_ref[...] = (y_ref[:, 3 * R :] - dot(y_ref[:, : 3 * R], x)).astype(BF16)


def whole(kernel, outs, scratch, operands):
    smem = pl.BlockSpec(memory_space=pltpu.SMEM)
    vmem = pl.BlockSpec(memory_space=pltpu.VMEM)
    return pl.pallas_call(
        kernel,
        in_specs=[smem] + [vmem] * (len(operands) - 1),
        out_specs=[vmem] * len(outs) if len(outs) > 1 else vmem,
        out_shape=outs if len(outs) > 1 else outs[0],
        scratch_shapes=scratch,
        compiler_params=pltpu.CompilerParams(vmem_limit_bytes=VMEM_BYTES),
    )(*operands)


def local(coupling, rhs, left_factors, right_factors):
    leaves, rows = lax.axis_size("leaf"), lax.axis_size("row")
    leaf, row = lax.axis_index("leaf"), lax.axis_index("row")
    where = jnp.stack([row % 2, leaf % 2, leaf // 2 % 4]).astype(jnp.int32)
    swap = [(i, i ^ 1) for i in range(rows)]
    own = jnp.concatenate([left_factors[0], rhs[0]], axis=1)
    gathered = lax.all_gather(own, "row", axis=0, tiled=True)
    y, keep, send = apply_leaf(where, coupling[0], gathered, own, right_factors[0])
    half, width = keep.shape
    keep = keep + lax.ppermute(send, "row", swap)
    quarter = half // 4
    same_core = [list(range(c, rows, 2)) for c in range(2)]
    pieces = lax.all_to_all(keep.reshape(4, quarter, width), "row", 0, 0, tiled=True, axis_index_groups=same_core)
    piece = jnp.sum(pieces, axis=0)
    column = [
        [(2 * g + low) * rows + 2 * high + c for low in range(2) for high in range(rows // 2)]
        for g in range(leaves // 2)
        for c in range(2)
    ]
    mine = lax.all_gather(piece, ("leaf", "row"), axis=0, tiled=True, axis_index_groups=column)
    mine = mine.reshape(2, half, width)
    others = lax.ppermute(mine, "row", swap)
    coef, part = whole(
        first_level,
        [jax.ShapeDtypeStruct((R, 3 * R), F32), jax.ShapeDtypeStruct((R, 3 * R), F32)],
        [pltpu.VMEM((2, 2, half, width), F32), pltpu.VMEM((R, R), F32)],
        (where, mine, others),
    )
    window = [[8 * g + 2 * n + low for n in range(4)] for g in range(leaves // 8) for low in range(2)]
    nodes = lax.all_gather(part, "leaf", axis=0, axis_index_groups=window)
    others = lax.ppermute(nodes, "row", swap)
    out = whole(
        last_levels,
        [jax.ShapeDtypeStruct((y.shape[0], R), BF16)],
        [
            pltpu.VMEM((2, 4, R, 3 * R), F32),
            pltpu.VMEM((2, R, 2 * R), F32),
            pltpu.VMEM((R, R), F32),
            pltpu.VMEM((R, R), F32),
        ],
        (where, nodes, others, coef, y),
    )
    return out[None]


def solution(mesh):
    spec = P("leaf", "row", None)
    return jax.shard_map(local, mesh=mesh, in_specs=(spec,) * 4, out_specs=spec, check_vma=False)
```

```python
import functools

import jax
import jax.numpy as jnp
from jax import lax
from jax.experimental import pallas as pl
from jax.experimental.pallas import tpu as pltpu
from jax.sharding import PartitionSpec as P

R = 128
BLOCK = 512
F32 = jnp.float32
BF16 = jnp.bfloat16
VMEM_BYTES = 48 * 1024 * 1024


def dot(a, b):
    return jnp.dot(a, b, precision=lax.Precision.HIGHEST, preferred_element_type=F32)


def invert(s, right, c_ref, p_ref):
    eye = (lax.broadcasted_iota(jnp.int32, (R, R), 0) == lax.broadcasted_iota(jnp.int32, (R, R), 1)).astype(F32)
    a = eye - s
    one = jnp.max(jnp.sum(jnp.abs(a), axis=0))
    most = jnp.max(jnp.sum(jnp.abs(a), axis=1))
    p_ref[...] = (a / one).T / most

    def again(state):
        step, old, new = state
        still = jnp.logical_or(new > 0.01, new < 0.25 * old)
        return jnp.logical_and(step < 200, jnp.logical_and(new > 1e-12, still))

    def newton(state):
        x = p_ref[...]
        res = eye - dot(a, x)
        p_ref[...] = x + dot(x, res)
        return (state[0] + 1, state[2], jnp.sum(res * res))

    lax.while_loop(again, newton, (jnp.int32(0), jnp.float32(1e30), jnp.float32(1e29)))
    x = p_ref[...]
    c_ref[...] = dot(x, right)
    for _ in range(2):
        c_ref[...] = c_ref[...] + dot(x, right - dot(a, c_ref[...]))


def solve(systems):
    left = jnp.float32(0)
    grown = jnp.float32(0)
    for s, right, c_ref, p_ref in systems:
        c = right + dot(s, right)
        p = dot(s, s)
        for _ in range(2):
            c = c + dot(p, c)
            p = dot(p, p)
        c_ref[...] = c
        p_ref[...] = p
        left = jnp.maximum(left, jnp.sum(p * p))
        grown = jnp.maximum(grown, jnp.sum(s * s))
    good = jnp.logical_and(left < 0.25, grown < 64.0)

    @pl.when(good)
    def _():
        def more(_):
            size = jnp.float32(0)
            for _, _, c_ref, p_ref in systems:
                q = p_ref[...]
                c_ref[...] = c_ref[...] + dot(q, c_ref[...])
                q = dot(q, q)
                p_ref[...] = q
                size = jnp.maximum(size, jnp.sum(q * q))
            return size

        lax.while_loop(lambda size: size > 1e-15, more, left)

    @pl.when(jnp.logical_not(good))
    def _():
        for system in systems:
            invert(*system)


def column(row):
    return pl.ds(pl.multiple_of(row * BLOCK, BLOCK), BLOCK)


def term(block_ref, row, cols_ref):
    return jnp.dot(block_ref[:, column(row)], cols_ref[...], preferred_element_type=F32)


def start_kernel(where_ref, block_ref, own_ref, y_ref):
    y_ref[...] = own_ref[...].astype(F32) + term(block_ref, where_ref[3], own_ref)


def more_kernel(rows, where_ref, block_ref, *refs):
    *cols_refs, before_ref, y_ref = refs
    y_ref[...] = before_ref[...] + term(block_ref, where_ref[rows[0]], cols_refs[0])
    for row, cols_ref in zip(rows[1:], cols_refs[1:]):
        y_ref[...] += term(block_ref, where_ref[row], cols_ref)


def far_kernel(where_ref, block_ref, far_ref, next_near_ref, swapped_ref, before_ref, v_ref, y_ref, keep_ref, send_ref, gram_ref):
    core = where_ref[0]
    y_ref[...] = before_ref[...] + term(block_ref, where_ref[9], far_ref)
    y_ref[...] += term(block_ref, where_ref[8], next_near_ref)
    y_ref[...] += term(block_ref, where_ref[10], swapped_ref)
    rest = y_ref[...]
    total = None
    for _ in range(2):
        piece = rest.astype(BF16)
        rest = rest - piece.astype(F32)
        part = lax.dot_general(v_ref[...], piece, (((0,), (0,)), ((), ())), preferred_element_type=F32)
        total = part if total is None else total + part
    gram_ref[...] = total.reshape(gram_ref.shape)
    keep_ref[...] = gram_ref[core]
    send_ref[...] = gram_ref[1 - core]


def first_level(where_ref, own_ref, other_ref, coef_ref, half_ref, full_ref, p_ref):
    core, leaf = where_ref[0], where_ref[1]
    full_ref[core] = own_ref[...]
    full_ref[1 - core] = other_ref[...]
    a, b = leaf, 1 - leaf
    lead = full_ref[0, a, :R, :]
    product = dot(full_ref[0, b, :R, :R], lead)
    right = full_ref[0, b, :R, R:] - product[:, R:]
    solve([(product[:, :R], right, coef_ref, p_ref)])
    coef = coef_ref[...]
    coef_b = lead[:, R:] - dot(lead[:, :R], coef)

    @pl.when(core == 0)
    def _():
        total = None
        for node, c in ((a, coef), (b, coef_b)):
            rows = jnp.concatenate([full_ref[0, node, R:, :], full_ref[1, node, :64, :]], axis=0)
            term = rows[:, R:] - dot(rows[:, :R], c)
            total = term if total is None else total + term
        half_ref[...] = total

    @pl.when(core == 1)
    def _():
        total = None
        for node, c in ((a, coef), (b, coef_b)):
            rows = full_ref[1, node, 64:, :]
            term = rows[:, R:] - dot(rows[:, :R], c)
            total = term if total is None else total + term
        half_ref[...] = total


def last_levels(where_ref, own_ref, other_ref, coef_ref, y_ref, out_ref, full_ref, c_ref, d_ref, p_ref):
    core, node = where_ref[0], where_ref[2]
    full_ref[core] = own_ref[...]
    full_ref[1 - core] = other_ref[...]

    pairs = ((node, node ^ 1), (node ^ 2, node ^ 3))
    systems = []
    for index, (a, b) in enumerate(pairs):
        product = dot(full_ref[0, b, :, :R], full_ref[0, a])
        right = full_ref[0, b, :, R:] - product[:, R:]
        systems.append((product[:, :R], right, c_ref.at[index], p_ref.at[index]))
    solve(systems)
    sums = []
    for index, (a, b) in enumerate(pairs):
        coef_a = c_ref[index]
        coef_b = full_ref[0, a, :, R:] - dot(full_ref[0, a, :, :R], coef_a)
        total = None
        for place, c in ((a, coef_a), (b, coef_b)):
            part = full_ref[1, place, :, R:] - dot(full_ref[1, place, :, :R], c)
            total = part if total is None else total + part
        sums.append(total)
    own, other = sums
    product = dot(other[:, :R], own)
    solve([(product[:, :R], other[:, R:] - product[:, R:], d_ref, p_ref.at[0])])
    x2 = d_ref[...]
    c1 = c_ref[0]
    c0 = coef_ref[...]
    x1 = c1[:, R:] - dot(c1[:, :R], x2)
    x0 = c0[:, 2 * R :] - dot(c0[:, :R], x1) - dot(c0[:, R : 2 * R], x2)
    x = jnp.concatenate([x0, x1, x2], axis=0)
    out_ref[...] = (y_ref[:, 3 * R :] - dot(y_ref[:, : 3 * R], x)).astype(BF16)


def whole(kernel, outs, scratch, operands):
    smem = pl.BlockSpec(memory_space=pltpu.SMEM)
    vmem = pl.BlockSpec(memory_space=pltpu.VMEM)
    return pl.pallas_call(
        kernel,
        in_specs=[smem] + [vmem] * (len(operands) - 1),
        out_specs=[vmem] * len(outs) if len(outs) > 1 else vmem,
        out_shape=outs if len(outs) > 1 else outs[0],
        scratch_shapes=scratch,
        cost_estimate=pl.CostEstimate(flops=10**9, bytes_accessed=10**7, transcendentals=0),
        compiler_params=pltpu.CompilerParams(vmem_limit_bytes=VMEM_BYTES),
    )(*operands)


def local(coupling, rhs, left_factors, right_factors):
    leaves, rows = lax.axis_size("leaf"), lax.axis_size("row")
    leaf, row = lax.axis_index("leaf"), lax.axis_index("row")
    core, high, ring = row % 2, row // 2, rows // 2
    behind = (high + 2 * core - 1) % ring * 2
    ahead = (high - 2 * core + 1) % ring * 2
    far = (high + 2) % ring * 2
    where = [core, leaf % 2, leaf // 2 % 4, row, row ^ 1]
    where += [behind + core, behind + 1 - core, ahead + 1 - core, ahead + core, far + core, far + 1 - core]
    where = jnp.stack(where).astype(jnp.int32)
    swap = [(i, i ^ 1) for i in range(rows)]
    onward = [(i, (i + 2 - 4 * (i % 2)) % rows) for i in range(rows)]

    def move(value, way):
        return lax.ppermute(value, "row", way)

    block, v = coupling[0], right_factors[0]
    own = jnp.concatenate([left_factors[0], rhs[0]], axis=1)
    width, half = own.shape[1], v.shape[1] // 2
    y_shape = jax.ShapeDtypeStruct((BLOCK, width), F32)
    g_shape = jax.ShapeDtypeStruct((half, width), F32)

    def more(rows, cols, before):
        return whole(functools.partial(more_kernel, rows), [y_shape], [], (where, block, *cols, before))

    near = move(own, onward)
    own_s = move(own, swap)
    next_near = move(own_s, onward)
    y = whole(start_kernel, [y_shape], [], (where, block, own))
    far = move(near, onward)
    near_s = move(near, swap)
    y = more((4, 5), (own_s, near), y)
    y = more((6, 7), (next_near, near_s), y)
    far, next_near, y = lax.optimization_barrier((far, next_near, y))
    y, keep, send = whole(
        far_kernel,
        [y_shape, g_shape, g_shape],
        [pltpu.VMEM((2, half, width), F32)],
        (where, block, far, move(next_near, swap), move(far, swap), y, v),
    )
    keep = keep + move(send, swap)
    quarter = half // 4
    same_core = [list(range(c, rows, 2)) for c in range(2)]
    pieces = lax.all_to_all(keep.reshape(4, quarter, width), "row", 0, 0, tiled=True, axis_index_groups=same_core)
    piece = jnp.sum(pieces, axis=0)
    sibling = lax.ppermute(piece, "leaf", [(i, i ^ 1) for i in range(leaves)])
    low = leaf % 2
    both = jnp.stack([jnp.where(low == 0, piece, sibling), jnp.where(low == 0, sibling, piece)])
    mine = lax.all_gather(both, "row", axis=1, tiled=True, axis_index_groups=same_core)
    mine = mine.reshape(2, half, width)
    others = lax.ppermute(mine, "row", swap)
    coef, part = whole(
        first_level,
        [jax.ShapeDtypeStruct((R, 3 * R), F32), jax.ShapeDtypeStruct((R, 3 * R), F32)],
        [pltpu.VMEM((2, 2, half, width), F32), pltpu.VMEM((R, R), F32)],
        (where, mine, others),
    )
    window = [[8 * g + 2 * n + low for n in range(4)] for g in range(leaves // 8) for low in range(2)]
    nodes = lax.all_gather(part, "leaf", axis=0, axis_index_groups=window)
    others = lax.ppermute(nodes, "row", swap)
    out = whole(
        last_levels,
        [jax.ShapeDtypeStruct((y.shape[0], R), BF16)],
        [
            pltpu.VMEM((2, 4, R, 3 * R), F32),
            pltpu.VMEM((2, R, 2 * R), F32),
            pltpu.VMEM((R, R), F32),
            pltpu.VMEM((2, R, R), F32),
        ],
        (where, nodes, others, coef, y),
    )
    return out[None]


def solution(mesh):
    spec = P("leaf", "row", None)
    return jax.shard_map(local, mesh=mesh, in_specs=(spec,) * 4, out_specs=spec, check_vma=False)
```

```python
import functools

import jax
import jax.numpy as jnp
from jax import lax
from jax.experimental import pallas as pl
from jax.experimental.pallas import tpu as pltpu
from jax.sharding import PartitionSpec as P

R = 128
BLOCK = 512
F32 = jnp.float32
BF16 = jnp.bfloat16
VMEM_BYTES = 48 * 1024 * 1024


def dot(a, b):
    return jnp.dot(a, b, precision=lax.Precision.HIGHEST, preferred_element_type=F32)


def invert(s, right, c_ref, p_ref):
    eye = (lax.broadcasted_iota(jnp.int32, (R, R), 0) == lax.broadcasted_iota(jnp.int32, (R, R), 1)).astype(F32)
    a = eye - s
    one = jnp.max(jnp.sum(jnp.abs(a), axis=0))
    most = jnp.max(jnp.sum(jnp.abs(a), axis=1))
    p_ref[...] = (a / one).T / most

    def again(state):
        step, old, new = state
        still = jnp.logical_or(new > 0.01, new < 0.25 * old)
        return jnp.logical_and(step < 200, jnp.logical_and(new > 1e-12, still))

    def newton(state):
        x = p_ref[...]
        res = eye - dot(a, x)
        p_ref[...] = x + dot(x, res)
        return (state[0] + 1, state[2], jnp.sum(res * res))

    lax.while_loop(again, newton, (jnp.int32(0), jnp.float32(1e30), jnp.float32(1e29)))
    x = p_ref[...]
    c_ref[...] = dot(x, right)
    for _ in range(2):
        c_ref[...] = c_ref[...] + dot(x, right - dot(a, c_ref[...]))


def solve(systems):
    left = jnp.float32(0)
    grown = jnp.float32(0)
    for s, right, c_ref, p_ref in systems:
        c = right + dot(s, right)
        p = dot(s, s)
        for _ in range(2):
            c = c + dot(p, c)
            p = dot(p, p)
        c_ref[...] = c
        p_ref[...] = p
        left = jnp.maximum(left, jnp.sum(p * p))
        grown = jnp.maximum(grown, jnp.sum(s * s))
    good = jnp.logical_and(left < 0.25, grown < 64.0)

    @pl.when(good)
    def _():
        def more(_):
            size = jnp.float32(0)
            for _, _, c_ref, p_ref in systems:
                q = p_ref[...]
                c_ref[...] = c_ref[...] + dot(q, c_ref[...])
                q = dot(q, q)
                p_ref[...] = q
                size = jnp.maximum(size, jnp.sum(q * q))
            return size

        lax.while_loop(lambda size: size > 1e-13, more, left)

    @pl.when(jnp.logical_not(good))
    def _():
        for system in systems:
            invert(*system)


def column(row):
    return pl.ds(pl.multiple_of(row * BLOCK, BLOCK), BLOCK)


def term(block_ref, row, cols_ref):
    return jnp.dot(block_ref[:, column(row)], cols_ref[...], preferred_element_type=F32)


def start_kernel(where_ref, block_ref, own_ref, y_ref):
    y_ref[...] = own_ref[...].astype(F32) + term(block_ref, where_ref[3], own_ref)


def more_kernel(rows, where_ref, block_ref, *refs):
    *cols_refs, before_ref, y_ref = refs
    y_ref[...] = before_ref[...] + term(block_ref, where_ref[rows[0]], cols_refs[0])
    for row, cols_ref in zip(rows[1:], cols_refs[1:]):
        y_ref[...] += term(block_ref, where_ref[row], cols_ref)


def far_kernel(where_ref, block_ref, next_near_ref, far_ref, before_ref, v_ref, y_ref, keep_ref, send_ref, gram_ref):
    core = where_ref[0]
    y_ref[...] = before_ref[...] + term(block_ref, where_ref[8], next_near_ref)
    y_ref[...] += term(block_ref, where_ref[10], far_ref)
    rest = y_ref[...]
    total = None
    for _ in range(2):
        piece = rest.astype(BF16)
        rest = rest - piece.astype(F32)
        part = lax.dot_general(v_ref[...], piece, (((0,), (0,)), ((), ())), preferred_element_type=F32)
        total = part if total is None else total + part
    gram_ref[...] = total
    for part_ref, c in ((keep_ref, core), (send_ref, 1 - core)):
        part_ref[: R // 2, :] = gram_ref[pl.ds(pl.multiple_of(c * (R // 2), R // 2), R // 2), :]
        part_ref[R // 2 :, :] = gram_ref[pl.ds(pl.multiple_of(R + c * R, R), R), :]


def first_level(own_ref, pair_ref, coef_ref, half_ref, p_ref):
    lead, sibling = (jnp.concatenate([pair_ref[0, node], pair_ref[1, node]], axis=0) for node in range(2))
    product = dot(sibling[:, :R], lead)
    solve([(product[:, :R], sibling[:, R:] - product[:, R:], coef_ref, p_ref)])
    coef = coef_ref[...]
    coef_b = lead[:, R:] - dot(lead[:, :R], coef)
    total = None
    for node, c in ((0, coef), (1, coef_b)):
        part = own_ref[node, R // 2 :, R:] - dot(own_ref[node, R // 2 :, :R], c)
        total = part if total is None else total + part
    half_ref[...] = total


def last_levels(where_ref, own_ref, other_ref, *refs):
    @pl.when(where_ref[0] == 0)
    def _():
        last_body(where_ref, own_ref, other_ref, *refs)

    @pl.when(where_ref[0] == 1)
    def _():
        last_body(where_ref, other_ref, own_ref, *refs)


def last_body(where_ref, v1_ref, v2_ref, coef_ref, y_ref, out_ref, c_ref, d_ref, p_ref):
    node = where_ref[2]
    pairs = ((node, node ^ 1), (node ^ 2, node ^ 3))
    systems = []
    for index, (a, b) in enumerate(pairs):
        product = dot(v1_ref[b, :, :R], v1_ref[a])
        right = v1_ref[b, :, R:] - product[:, R:]
        systems.append((product[:, :R], right, c_ref.at[index], p_ref.at[index]))
    solve(systems)
    sums = []
    for index, (a, b) in enumerate(pairs):
        coef_a = c_ref[index]
        coef_b = v1_ref[a, :, R:] - dot(v1_ref[a, :, :R], coef_a)
        total = None
        for place, c in ((a, coef_a), (b, coef_b)):
            part = v2_ref[place, :, R:] - dot(v2_ref[place, :, :R], c)
            total = part if total is None else total + part
        sums.append(total)
    own, other = sums
    product = dot(other[:, :R], own)
    solve([(product[:, :R], other[:, R:] - product[:, R:], d_ref, p_ref.at[0])])
    x2 = d_ref[...]
    c1 = c_ref[0]
    c0 = coef_ref[...]
    x1 = c1[:, R:] - dot(c1[:, :R], x2)
    x0 = c0[:, 2 * R :] - dot(c0[:, :R], x1) - dot(c0[:, R : 2 * R], x2)
    x = jnp.concatenate([x0, x1, x2], axis=0)
    out_ref[...] = (y_ref[:, 3 * R :] - dot(y_ref[:, : 3 * R], x)).astype(BF16)


def whole(kernel, outs, scratch, operands):
    smem = pl.BlockSpec(memory_space=pltpu.SMEM)
    vmem = pl.BlockSpec(memory_space=pltpu.VMEM)
    return pl.pallas_call(
        kernel,
        in_specs=[smem if x.ndim == 1 else vmem for x in operands],
        out_specs=[vmem] * len(outs) if len(outs) > 1 else vmem,
        out_shape=outs if len(outs) > 1 else outs[0],
        scratch_shapes=scratch,
        cost_estimate=pl.CostEstimate(flops=10**9, bytes_accessed=10**7, transcendentals=0),
        compiler_params=pltpu.CompilerParams(vmem_limit_bytes=VMEM_BYTES),
    )(*operands)


def local(coupling, rhs, left_factors, right_factors):
    leaves, rows = lax.axis_size("leaf"), lax.axis_size("row")
    leaf, row = lax.axis_index("leaf"), lax.axis_index("row")
    core, high, ring = row % 2, row // 2, rows // 2
    behind = (high + 2 * core - 1) % ring * 2
    ahead = (high - 2 * core + 1) % ring * 2
    far = (high + 2) % ring * 2
    where = [core, leaf % 2, leaf // 2 % 4, row, row ^ 1]
    where += [behind + core, behind + 1 - core, ahead + 1 - core, ahead + core, far + core, far + 1 - core]
    where = jnp.stack(where).astype(jnp.int32)
    swap = [(i, i ^ 1) for i in range(rows)]
    onward = [(i, (i + 2 - 4 * (i % 2)) % rows) for i in range(rows)]

    def move(value, way):
        return lax.ppermute(value, "row", way)

    block, v = coupling[0], right_factors[0]
    own = jnp.concatenate([left_factors[0], rhs[0]], axis=1)
    width, half = own.shape[1], v.shape[1] // 2
    y_shape = jax.ShapeDtypeStruct((BLOCK, width), F32)
    g_shape = jax.ShapeDtypeStruct((half, width), F32)

    def more(rows, cols, before):
        return whole(functools.partial(more_kernel, rows), [y_shape], [], (where, block, *cols, before))

    near = move(own, onward)
    own_s = move(own, swap)
    y = whole(start_kernel, [y_shape], [], (where, block, own))
    y = more((4,), (own_s,), y)
    own_s, y = lax.optimization_barrier((own_s, y))
    next_near = move(own_s, onward)
    far = move(near, onward)
    y = more((5,), (near,), y)
    near, y = lax.optimization_barrier((near, y))
    near_s = move(near, swap)
    y = more((6,), (next_near,), y)
    next_near, y = lax.optimization_barrier((next_near, y))
    next_near_s = move(next_near, swap)
    far_s = move(far, swap)
    y = more((7, 9), (near_s, far), y)
    y, keep, send = whole(
        far_kernel,
        [y_shape, g_shape, g_shape],
        [pltpu.VMEM((2 * half, width), F32)],
        (where, block, next_near_s, far_s, y, v),
    )
    keep = keep + move(send, swap)
    quarter = half // 4
    same_core = [list(range(c, rows, 2)) for c in range(2)]
    pieces = lax.all_to_all(keep.reshape(4, quarter, width), "row", 0, 0, tiled=True, axis_index_groups=same_core)
    piece = jnp.sum(pieces, axis=0)
    sibling = lax.ppermute(piece, "leaf", [(i, i ^ 1) for i in range(leaves)])
    both = jnp.stack([piece, sibling])
    mine = lax.all_gather(both, "row", axis=1, tiled=True, axis_index_groups=same_core)
    mine = mine.reshape(2, half, width)
    chip = [[2 * i, 2 * i + 1] for i in range(rows // 2)]
    pair = lax.all_gather(mine[:, : R // 2], "row", axis=0, axis_index_groups=chip)
    coef, part = whole(
        first_level,
        [jax.ShapeDtypeStruct((R, 3 * R), F32), jax.ShapeDtypeStruct((R, 3 * R), F32)],
        [pltpu.VMEM((R, R), F32)],
        (mine, pair),
    )
    window = [[8 * g + 2 * n + low for n in range(4)] for g in range(leaves // 8) for low in range(2)]
    nodes = lax.all_gather(part, "leaf", axis=0, axis_index_groups=window)
    others = move(nodes, swap)
    out = whole(
        last_levels,
        [jax.ShapeDtypeStruct((y.shape[0], R), BF16)],
        [
            pltpu.VMEM((2, R, 2 * R), F32),
            pltpu.VMEM((R, R), F32),
            pltpu.VMEM((2, R, R), F32),
        ],
        (where, nodes, others, coef, y),
    )
    return out[None]


def solution(mesh):
    spec = P("leaf", "row", None)
    return jax.shard_map(local, mesh=mesh, in_specs=(spec,) * 4, out_specs=spec, check_vma=False)
```

```python
import functools

import jax
import jax.numpy as jnp
from jax import lax
from jax.experimental import pallas as pl
from jax.experimental.pallas import tpu as pltpu
from jax.sharding import PartitionSpec as P

R = 128
BLOCK = 512
F32 = jnp.float32
BF16 = jnp.bfloat16
VMEM_BYTES = 16 * 1024 * 1024


def dot(a, b):
    return jnp.dot(a, b, precision=lax.Precision.HIGHEST, preferred_element_type=F32)


def invert(s, right, c_ref, p_ref):
    eye = (lax.broadcasted_iota(jnp.int32, (R, R), 0) == lax.broadcasted_iota(jnp.int32, (R, R), 1)).astype(F32)
    a = eye - s
    one = jnp.max(jnp.sum(jnp.abs(a), axis=0))
    most = jnp.max(jnp.sum(jnp.abs(a), axis=1))
    p_ref[...] = (a / one).T / most

    def again(state):
        step, old, new = state
        still = jnp.logical_or(new > 0.01, new < 0.25 * old)
        return jnp.logical_and(step < 200, jnp.logical_and(new > 1e-12, still))

    def newton(state):
        x = p_ref[...]
        res = eye - dot(a, x)
        p_ref[...] = x + dot(x, res)
        return (state[0] + 1, state[2], jnp.sum(res * res))

    lax.while_loop(again, newton, (jnp.int32(0), jnp.float32(1e30), jnp.float32(1e29)))
    x = p_ref[...]
    c_ref[...] = dot(x, right)
    for _ in range(2):
        c_ref[...] = c_ref[...] + dot(x, right - dot(a, c_ref[...]))


def solve(systems):
    left = jnp.float32(0)
    grown = jnp.float32(0)
    for s, right, c_ref, p_ref in systems:
        c = right + dot(s, right)
        p = dot(s, s)
        for _ in range(2):
            c = c + dot(p, c)
            p = dot(p, p)
        c_ref[...] = c
        p_ref[...] = p
        left = jnp.maximum(left, jnp.sum(p * p))
        grown = jnp.maximum(grown, jnp.sum(s * s))
    good = jnp.logical_and(left < 0.25, grown < 64.0)

    @pl.when(good)
    def _():
        def more(_):
            size = jnp.float32(0)
            for _, _, c_ref, p_ref in systems:
                q = p_ref[...]
                c_ref[...] = c_ref[...] + dot(q, c_ref[...])
                q = dot(q, q)
                p_ref[...] = q
                size = jnp.maximum(size, jnp.sum(q * q))
            return size

        lax.while_loop(lambda size: size > 1e-13, more, left)

    @pl.when(jnp.logical_not(good))
    def _():
        for system in systems:
            invert(*system)


def column(row):
    return pl.ds(pl.multiple_of(row * BLOCK, BLOCK), BLOCK)


def terms(where_ref, block_ref, rows, cols_refs):
    blocks = jnp.concatenate([block_ref[:, column(where_ref[row])] for row in rows], axis=1)
    cols = jnp.concatenate([cols_ref[...] for cols_ref in cols_refs], axis=0)
    return jnp.dot(blocks, cols, preferred_element_type=F32)


def start_kernel(where_ref, block_ref, own_ref, y_ref):
    y_ref[...] = own_ref[...].astype(F32) + terms(where_ref, block_ref, (3,), (own_ref,))


def more_kernel(rows, where_ref, block_ref, *refs):
    *cols_refs, before_ref, y_ref = refs
    y_ref[...] = before_ref[...] + terms(where_ref, block_ref, rows, cols_refs)


def far_kernel(where_ref, block_ref, next_near_ref, far_ref, before_ref, v_ref, y_ref, keep_ref, send_ref, gram_ref):
    core = where_ref[0]
    y_ref[...] = before_ref[...] + terms(where_ref, block_ref, (8, 10), (next_near_ref, far_ref))
    rest = y_ref[...]
    total = None
    for _ in range(2):
        piece = rest.astype(BF16)
        rest = rest - piece.astype(F32)
        part = lax.dot_general(v_ref[...], piece, (((0,), (0,)), ((), ())), preferred_element_type=F32)
        total = part if total is None else total + part
    gram_ref[...] = total
    for part_ref, c in ((keep_ref, core), (send_ref, 1 - core)):
        part_ref[: R // 2, :] = gram_ref[pl.ds(pl.multiple_of(c * (R // 2), R // 2), R // 2), :]
        part_ref[R // 2 :, :] = gram_ref[pl.ds(pl.multiple_of(R + c * R, R), R), :]


def first_level(own_ref, pair_ref, coef_ref, half_ref, p_ref):
    lead, sibling = (jnp.concatenate([pair_ref[0, node], pair_ref[1, node]], axis=0) for node in range(2))
    product = dot(sibling[:, :R], lead)
    solve([(product[:, :R], sibling[:, R:] - product[:, R:], coef_ref, p_ref)])
    coef = coef_ref[...]
    coef_b = lead[:, R:] - dot(lead[:, :R], coef)
    total = None
    for node, c in ((0, coef), (1, coef_b)):
        part = own_ref[node, R // 2 :, R:] - dot(own_ref[node, R // 2 :, :R], c)
        total = part if total is None else total + part
    half_ref[...] = total


def last_levels(where_ref, own_ref, other_ref, *refs):
    @pl.when(where_ref[0] == 0)
    def _():
        last_body(where_ref, own_ref, other_ref, *refs)

    @pl.when(where_ref[0] == 1)
    def _():
        last_body(where_ref, other_ref, own_ref, *refs)


def last_body(where_ref, v1_ref, v2_ref, coef_ref, y_ref, out_ref, c_ref, d_ref, p_ref):
    node = where_ref[2]
    pairs = ((node, node ^ 1), (node ^ 2, node ^ 3))
    systems = []
    for index, (a, b) in enumerate(pairs):
        product = dot(v1_ref[b, :, :R], v1_ref[a])
        right = v1_ref[b, :, R:] - product[:, R:]
        systems.append((product[:, :R], right, c_ref.at[index], p_ref.at[index]))
    solve(systems)
    sums = []
    for index, (a, b) in enumerate(pairs):
        coef_a = c_ref[index]
        coef_b = v1_ref[a, :, R:] - dot(v1_ref[a, :, :R], coef_a)
        total = None
        for place, c in ((a, coef_a), (b, coef_b)):
            part = v2_ref[place, :, R:] - dot(v2_ref[place, :, :R], c)
            total = part if total is None else total + part
        sums.append(total)
    own, other = sums
    product = dot(other[:, :R], own)
    solve([(product[:, :R], other[:, R:] - product[:, R:], d_ref, p_ref.at[0])])
    x2 = d_ref[...]
    c1 = c_ref[0]
    c0 = coef_ref[...]
    x1 = c1[:, R:] - dot(c1[:, :R], x2)
    x0 = c0[:, 2 * R :] - dot(c0[:, :R], x1) - dot(c0[:, R : 2 * R], x2)
    x = jnp.concatenate([x0, x1, x2], axis=0)
    out_ref[...] = (y_ref[:, 3 * R :] - dot(y_ref[:, : 3 * R], x)).astype(BF16)


def whole(kernel, outs, scratch, operands):
    smem = pl.BlockSpec(memory_space=pltpu.SMEM)
    vmem = pl.BlockSpec(memory_space=pltpu.VMEM)
    return pl.pallas_call(
        kernel,
        in_specs=[smem if x.ndim == 1 else vmem for x in operands],
        out_specs=[vmem] * len(outs) if len(outs) > 1 else vmem,
        out_shape=outs if len(outs) > 1 else outs[0],
        scratch_shapes=scratch,
        cost_estimate=pl.CostEstimate(flops=10**9, bytes_accessed=10**7, transcendentals=0),
        compiler_params=pltpu.CompilerParams(vmem_limit_bytes=VMEM_BYTES),
    )(*operands)


def local(coupling, rhs, left_factors, right_factors):
    leaves, rows = lax.axis_size("leaf"), lax.axis_size("row")
    leaf, row = lax.axis_index("leaf"), lax.axis_index("row")
    core, high, ring = row % 2, row // 2, rows // 2
    behind = (high + 2 * core - 1) % ring * 2
    ahead = (high - 2 * core + 1) % ring * 2
    far = (high + 2) % ring * 2
    where = [core, leaf % 2, leaf // 2 % 4, row, row ^ 1]
    where += [behind + core, behind + 1 - core, ahead + 1 - core, ahead + core, far + core, far + 1 - core]
    where = jnp.stack(where).astype(jnp.int32)
    swap = [(i, i ^ 1) for i in range(rows)]
    onward = [(i, (i + 2 - 4 * (i % 2)) % rows) for i in range(rows)]

    def move(value, way):
        return lax.ppermute(value, "row", way)

    block, v = coupling[0], right_factors[0]
    own = jnp.concatenate([left_factors[0], rhs[0]], axis=1)
    width, half = own.shape[1], v.shape[1] // 2
    y_shape = jax.ShapeDtypeStruct((BLOCK, width), F32)
    g_shape = jax.ShapeDtypeStruct((half, width), F32)

    def more(rows, cols, before):
        return whole(functools.partial(more_kernel, rows), [y_shape], [], (where, block, *cols, before))

    near = move(own, onward)
    own_s = move(own, swap)
    y = whole(start_kernel, [y_shape], [], (where, block, own))
    y = more((4,), (own_s,), y)
    own_s, y = lax.optimization_barrier((own_s, y))
    next_near = move(own_s, onward)
    far = move(near, onward)
    y = more((5,), (near,), y)
    near, y = lax.optimization_barrier((near, y))
    near_s = move(near, swap)
    y = more((6,), (next_near,), y)
    next_near, y = lax.optimization_barrier((next_near, y))
    next_near_s = move(next_near, swap)
    far_s = move(far, swap)
    y = more((7, 9), (near_s, far), y)
    y, keep, send = whole(
        far_kernel,
        [y_shape, g_shape, g_shape],
        [pltpu.VMEM((2 * half, width), F32)],
        (where, block, next_near_s, far_s, y, v),
    )
    keep = keep + move(send, swap)
    quarter = half // 4
    same_core = [list(range(c, rows, 2)) for c in range(2)]
    pieces = lax.all_to_all(keep.reshape(4, quarter, width), "row", 0, 0, tiled=True, axis_index_groups=same_core)
    piece = jnp.sum(pieces, axis=0)
    sibling = lax.ppermute(piece, "leaf", [(i, i ^ 1) for i in range(leaves)])
    both = jnp.stack([piece, sibling])
    mine = lax.all_gather(both, "row", axis=1, tiled=True, axis_index_groups=same_core)
    mine = mine.reshape(2, half, width)
    chip = [[2 * i, 2 * i + 1] for i in range(rows // 2)]
    pair = lax.all_gather(mine[:, : R // 2], "row", axis=0, axis_index_groups=chip)
    coef, part = whole(
        first_level,
        [jax.ShapeDtypeStruct((R, 3 * R), F32), jax.ShapeDtypeStruct((R, 3 * R), F32)],
        [pltpu.VMEM((R, R), F32)],
        (mine, pair),
    )
    window = [[8 * g + 2 * n + low for n in range(4)] for g in range(leaves // 8) for low in range(2)]
    nodes = lax.all_gather(part, "leaf", axis=0, axis_index_groups=window)
    others = move(nodes, swap)
    out = whole(
        last_levels,
        [jax.ShapeDtypeStruct((y.shape[0], R), BF16)],
        [
            pltpu.VMEM((2, R, 2 * R), F32),
            pltpu.VMEM((R, R), F32),
            pltpu.VMEM((2, R, R), F32),
        ],
        (where, nodes, others, coef, y),
    )
    return out[None]


def solution(mesh):
    spec = P("leaf", "row", None)
    return jax.shard_map(local, mesh=mesh, in_specs=(spec,) * 4, out_specs=spec, check_vma=False)
```

```python
import functools

import jax
import jax.numpy as jnp
from jax import lax
from jax.experimental import pallas as pl
from jax.experimental.pallas import tpu as pltpu
from jax.sharding import PartitionSpec as P

R = 128
BLOCK = 512
F32 = jnp.float32
BF16 = jnp.bfloat16
VMEM_BYTES = 16 * 1024 * 1024


def dot(a, b):
    return jnp.dot(a, b, precision=lax.Precision.HIGHEST, preferred_element_type=F32)


def invert(s, right, c_ref, p_ref):
    eye = (lax.broadcasted_iota(jnp.int32, (R, R), 0) == lax.broadcasted_iota(jnp.int32, (R, R), 1)).astype(F32)
    a = eye - s
    one = jnp.max(jnp.sum(jnp.abs(a), axis=0))
    most = jnp.max(jnp.sum(jnp.abs(a), axis=1))
    p_ref[...] = (a / one).T / most

    def again(state):
        step, old, new = state
        still = jnp.logical_or(new > 0.01, new < 0.25 * old)
        return jnp.logical_and(step < 200, jnp.logical_and(new > 1e-12, still))

    def newton(state):
        x = p_ref[...]
        res = eye - dot(a, x)
        p_ref[...] = x + dot(x, res)
        return (state[0] + 1, state[2], jnp.sum(res * res))

    lax.while_loop(again, newton, (jnp.int32(0), jnp.float32(1e30), jnp.float32(1e29)))
    x = p_ref[...]
    c_ref[...] = dot(x, right)
    for _ in range(2):
        c_ref[...] = c_ref[...] + dot(x, right - dot(a, c_ref[...]))


def solve(systems):
    left = jnp.float32(0)
    grown = jnp.float32(0)
    for s, right, c_ref, p_ref in systems:
        c = right + dot(s, right)
        p = dot(s, s)
        for _ in range(2):
            c = c + dot(p, c)
            p = dot(p, p)
        c_ref[...] = c
        p_ref[...] = p
        left = jnp.maximum(left, jnp.sum(p * p))
        grown = jnp.maximum(grown, jnp.sum(s * s))
    good = jnp.logical_and(left < 0.25, grown < 64.0)

    @pl.when(good)
    def _():
        def more(_):
            size = jnp.float32(0)
            for _, _, c_ref, p_ref in systems:
                q = p_ref[...]
                c_ref[...] = c_ref[...] + dot(q, c_ref[...])
                q = dot(q, q)
                p_ref[...] = q
                size = jnp.maximum(size, jnp.sum(q * q))
            return size

        lax.while_loop(lambda size: size > 1e-13, more, left)

    @pl.when(jnp.logical_not(good))
    def _():
        for system in systems:
            invert(*system)


def column(row):
    return pl.ds(pl.multiple_of(row * BLOCK, BLOCK), BLOCK)


def terms(where_ref, block_ref, rows, cols_refs):
    blocks = jnp.concatenate([block_ref[:, column(where_ref[row])] for row in rows], axis=1)
    cols = jnp.concatenate([cols_ref[...] for cols_ref in cols_refs], axis=0)
    return jnp.dot(blocks, cols, preferred_element_type=F32)


def start_kernel(where_ref, block_ref, own_ref, y_ref):
    y_ref[...] = own_ref[...].astype(F32) + terms(where_ref, block_ref, (3,), (own_ref,))


def more_kernel(rows, where_ref, block_ref, *refs):
    *cols_refs, before_ref, y_ref = refs
    y_ref[...] = before_ref[...] + terms(where_ref, block_ref, rows, cols_refs)


def far_kernel(where_ref, block_ref, next_near_ref, far_ref, before_ref, v_ref, y_ref, keep_ref, send_ref, gram_ref):
    core = where_ref[0]
    y_ref[...] = before_ref[...] + terms(where_ref, block_ref, (8, 10), (next_near_ref, far_ref))
    rest = y_ref[...]
    total = None
    for _ in range(2):
        piece = rest.astype(BF16)
        rest = rest - piece.astype(F32)
        part = lax.dot_general(v_ref[...], piece, (((0,), (0,)), ((), ())), preferred_element_type=F32)
        total = part if total is None else total + part
    gram_ref[...] = total
    for part_ref, c in ((keep_ref, core), (send_ref, 1 - core)):
        part_ref[: R // 2, :] = gram_ref[pl.ds(pl.multiple_of(c * (R // 2), R // 2), R // 2), :]
        part_ref[R // 2 :, :] = gram_ref[pl.ds(pl.multiple_of(R + c * R, R), R), :]


def first_level(own_ref, pair_ref, coef_ref, half_ref, p_ref):
    lead, sibling = (jnp.concatenate([pair_ref[0, node], pair_ref[1, node]], axis=0) for node in range(2))
    product = dot(sibling[:, :R], lead)
    solve([(product[:, :R], sibling[:, R:] - product[:, R:], coef_ref, p_ref)])
    coef = coef_ref[...]
    coef_b = lead[:, R:] - dot(lead[:, :R], coef)
    total = None
    for node, c in ((0, coef), (1, coef_b)):
        part = own_ref[node, R // 2 :, R:] - dot(own_ref[node, R // 2 :, :R], c)
        total = part if total is None else total + part
    half_ref[...] = total


def last_levels(where_ref, own_ref, other_ref, *refs):
    @pl.when(where_ref[0] == 0)
    def _():
        last_body(where_ref, own_ref, other_ref, *refs)

    @pl.when(where_ref[0] == 1)
    def _():
        last_body(where_ref, other_ref, own_ref, *refs)


def last_body(where_ref, v1_ref, v2_ref, y_ref, out_ref, c_ref, d_ref, p_ref, z_ref):
    node = where_ref[2]
    pairs = ((node, node ^ 1), (node ^ 2, node ^ 3))
    systems = []
    for index, (a, b) in enumerate(pairs):
        product = dot(v1_ref[b, :, :R], v1_ref[a])
        right = v1_ref[b, :, R:] - product[:, R:]
        systems.append((product[:, :R], right, c_ref.at[index], p_ref.at[index]))
    solve(systems)
    sums = []
    for index, (a, b) in enumerate(pairs):
        coef_a = c_ref[index]
        coef_b = v1_ref[a, :, R:] - dot(v1_ref[a, :, :R], coef_a)
        total = None
        for place, c in ((a, coef_a), (b, coef_b)):
            part = v2_ref[place, :, R:] - dot(v2_ref[place, :, :R], c)
            total = part if total is None else total + part
        sums.append(total)
    own, other = sums
    z_ref[...] = y_ref[:, R:] - dot(y_ref[:, :R], c_ref[0])
    product = dot(other[:, :R], own)
    solve([(product[:, :R], other[:, R:] - product[:, R:], d_ref, p_ref.at[0])])
    out_ref[...] = (z_ref[:, R:] - dot(z_ref[:, :R], d_ref[...])).astype(BF16)


def lift_kernel(coef_ref, y_ref, out_ref):
    out_ref[...] = y_ref[:, R:] - dot(y_ref[:, :R], coef_ref[...])


def whole(kernel, outs, scratch, operands):
    smem = pl.BlockSpec(memory_space=pltpu.SMEM)
    vmem = pl.BlockSpec(memory_space=pltpu.VMEM)
    return pl.pallas_call(
        kernel,
        in_specs=[smem if x.ndim == 1 else vmem for x in operands],
        out_specs=[vmem] * len(outs) if len(outs) > 1 else vmem,
        out_shape=outs if len(outs) > 1 else outs[0],
        scratch_shapes=scratch,
        cost_estimate=pl.CostEstimate(flops=10**9, bytes_accessed=10**7, transcendentals=0),
        compiler_params=pltpu.CompilerParams(vmem_limit_bytes=VMEM_BYTES),
    )(*operands)


def local(coupling, rhs, left_factors, right_factors):
    leaves, rows = lax.axis_size("leaf"), lax.axis_size("row")
    leaf, row = lax.axis_index("leaf"), lax.axis_index("row")
    core, high, ring = row % 2, row // 2, rows // 2
    behind = (high + 2 * core - 1) % ring * 2
    ahead = (high - 2 * core + 1) % ring * 2
    far = (high + 2) % ring * 2
    where = [core, leaf % 2, leaf // 2 % 4, row, row ^ 1]
    where += [behind + core, behind + 1 - core, ahead + 1 - core, ahead + core, far + core, far + 1 - core]
    where = jnp.stack(where).astype(jnp.int32)
    swap = [(i, i ^ 1) for i in range(rows)]
    onward = [(i, (i + 2 - 4 * (i % 2)) % rows) for i in range(rows)]

    def move(value, way):
        return lax.ppermute(value, "row", way)

    block, v = coupling[0], right_factors[0]
    own = jnp.concatenate([left_factors[0], rhs[0]], axis=1)
    width, half = own.shape[1], v.shape[1] // 2
    y_shape = jax.ShapeDtypeStruct((BLOCK, width), F32)
    g_shape = jax.ShapeDtypeStruct((half, width), F32)

    def more(rows, cols, before):
        return whole(functools.partial(more_kernel, rows), [y_shape], [], (where, block, *cols, before))

    near = move(own, onward)
    own_s = move(own, swap)
    y = whole(start_kernel, [y_shape], [], (where, block, own))
    y = more((4,), (own_s,), y)
    own_s, y = lax.optimization_barrier((own_s, y))
    next_near = move(own_s, onward)
    far = move(near, onward)
    y = more((5,), (near,), y)
    near, y = lax.optimization_barrier((near, y))
    near_s = move(near, swap)
    y = more((6,), (next_near,), y)
    next_near, y = lax.optimization_barrier((next_near, y))
    next_near_s = move(next_near, swap)
    far_s = move(far, swap)
    y = more((7, 9), (near_s, far), y)
    y, keep, send = whole(
        far_kernel,
        [y_shape, g_shape, g_shape],
        [pltpu.VMEM((2 * half, width), F32)],
        (where, block, next_near_s, far_s, y, v),
    )
    keep = keep + move(send, swap)
    quarter = half // 4
    same_core = [list(range(c, rows, 2)) for c in range(2)]
    pieces = lax.all_to_all(keep.reshape(4, quarter, width), "row", 0, 0, tiled=True, axis_index_groups=same_core)
    piece = jnp.sum(pieces, axis=0)
    sibling = lax.ppermute(piece, "leaf", [(i, i ^ 1) for i in range(leaves)])
    both = jnp.stack([piece, sibling])
    mine = lax.all_gather(both, "row", axis=1, tiled=True, axis_index_groups=same_core)
    mine = mine.reshape(2, half, width)
    chip = [[2 * i, 2 * i + 1] for i in range(rows // 2)]
    pair = lax.all_gather(mine[:, : R // 2], "row", axis=0, axis_index_groups=chip)
    coef, part = whole(
        first_level,
        [jax.ShapeDtypeStruct((R, 3 * R), F32), jax.ShapeDtypeStruct((R, 3 * R), F32)],
        [pltpu.VMEM((R, R), F32)],
        (mine, pair),
    )
    window = [[8 * g + 2 * n + low for n in range(4)] for g in range(leaves // 8) for low in range(2)]
    nodes = lax.all_gather(part, "leaf", axis=0, axis_index_groups=window)
    others = move(nodes, swap)
    y = whole(lift_kernel, [jax.ShapeDtypeStruct((BLOCK, width - R), F32)], [], (coef, y))
    out = whole(
        last_levels,
        [jax.ShapeDtypeStruct((y.shape[0], R), BF16)],
        [
            pltpu.VMEM((2, R, 2 * R), F32),
            pltpu.VMEM((R, R), F32),
            pltpu.VMEM((2, R, R), F32),
            pltpu.VMEM((BLOCK, 2 * R), F32),
        ],
        (where, nodes, others, y),
    )
    return out[None]


def solution(mesh):
    spec = P("leaf", "row", None)
    return jax.shard_map(local, mesh=mesh, in_specs=(spec,) * 4, out_specs=spec, check_vma=False)
```

```python
import functools

import jax
import jax.numpy as jnp
from jax import lax
from jax.experimental import pallas as pl
from jax.experimental.pallas import tpu as pltpu
from jax.sharding import PartitionSpec as P

R = 128
BLOCK = 512
F32 = jnp.float32
BF16 = jnp.bfloat16
VMEM_BYTES = 16 * 1024 * 1024


def dot(a, b):
    return jnp.dot(a, b, precision=lax.Precision.HIGHEST, preferred_element_type=F32)


def invert(s, right, c_ref, p_ref):
    eye = (lax.broadcasted_iota(jnp.int32, (R, R), 0) == lax.broadcasted_iota(jnp.int32, (R, R), 1)).astype(F32)
    a = eye - s
    one = jnp.max(jnp.sum(jnp.abs(a), axis=0))
    most = jnp.max(jnp.sum(jnp.abs(a), axis=1))
    p_ref[...] = (a / one).T / most

    def again(state):
        step, old, new = state
        still = jnp.logical_or(new > 0.01, new < 0.25 * old)
        return jnp.logical_and(step < 200, jnp.logical_and(new > 1e-12, still))

    def newton(state):
        x = p_ref[...]
        res = eye - dot(a, x)
        p_ref[...] = x + dot(x, res)
        return (state[0] + 1, state[2], jnp.sum(res * res))

    lax.while_loop(again, newton, (jnp.int32(0), jnp.float32(1e30), jnp.float32(1e29)))
    x = p_ref[...]
    c_ref[...] = dot(x, right)
    for _ in range(2):
        c_ref[...] = c_ref[...] + dot(x, right - dot(a, c_ref[...]))


def solve(systems, rounds=2):
    left = jnp.float32(0)
    grown = jnp.float32(0)
    for s, right, c_ref, p_ref in systems:
        c = right + dot(s, right)
        p = dot(s, s)
        for _ in range(rounds):
            c = c + dot(p, c)
            p = dot(p, p)
        c_ref[...] = c
        p_ref[...] = p
        left = jnp.maximum(left, jnp.sum(p * p))
        grown = jnp.maximum(grown, jnp.sum(s * s))
    good = jnp.logical_and(left < 0.25, grown < 64.0)

    @pl.when(good)
    def _():
        def more(_):
            size = jnp.float32(0)
            for _, _, c_ref, p_ref in systems:
                q = p_ref[...]
                c_ref[...] = c_ref[...] + dot(q, c_ref[...])
                q = dot(q, q)
                p_ref[...] = q
                size = jnp.maximum(size, jnp.sum(q * q))
            return size

        lax.while_loop(lambda size: size > 1e-13, more, left)

    @pl.when(jnp.logical_not(good))
    def _():
        for system in systems:
            invert(*system)


def column(row):
    return pl.ds(pl.multiple_of(row * BLOCK, BLOCK), BLOCK)


def terms(where_ref, block_ref, rows, cols_refs):
    blocks = jnp.concatenate([block_ref[:, column(where_ref[row])] for row in rows], axis=1)
    cols = jnp.concatenate([cols_ref[...] for cols_ref in cols_refs], axis=0)
    return jnp.dot(blocks, cols, preferred_element_type=F32)


def start_kernel(where_ref, block_ref, own_ref, y_ref):
    y_ref[...] = own_ref[...].astype(F32) + terms(where_ref, block_ref, (3,), (own_ref,))


def more_kernel(rows, where_ref, block_ref, *refs):
    *cols_refs, before_ref, y_ref = refs
    y_ref[...] = before_ref[...] + terms(where_ref, block_ref, rows, cols_refs)


def far_kernel(where_ref, block_ref, next_near_ref, far_ref, before_ref, v_ref, y_ref, keep_ref, send_ref, gram_ref):
    core = where_ref[0]
    y_ref[...] = before_ref[...] + terms(where_ref, block_ref, (8, 10), (next_near_ref, far_ref))
    rest = y_ref[...]
    total = None
    for _ in range(2):
        piece = rest.astype(BF16)
        rest = rest - piece.astype(F32)
        part = lax.dot_general(v_ref[...], piece, (((0,), (0,)), ((), ())), preferred_element_type=F32)
        total = part if total is None else total + part
    gram_ref[...] = total
    for part_ref, c in ((keep_ref, core), (send_ref, 1 - core)):
        part_ref[: R // 2, :] = gram_ref[pl.ds(pl.multiple_of(c * (R // 2), R // 2), R // 2), :]
        part_ref[R // 2 :, :] = gram_ref[pl.ds(pl.multiple_of(R + c * R, R), R), :]


def first_level(own_ref, pair_ref, coef_ref, half_ref, p_ref):
    lead, sibling = (jnp.concatenate([pair_ref[0, node], pair_ref[1, node]], axis=0) for node in range(2))
    product = dot(sibling[:, :R], lead)
    solve([(product[:, :R], sibling[:, R:] - product[:, R:], coef_ref, p_ref)])
    coef = coef_ref[...]
    coef_b = lead[:, R:] - dot(lead[:, :R], coef)
    total = None
    for node, c in ((0, coef), (1, coef_b)):
        part = own_ref[node, R // 2 :, R:] - dot(own_ref[node, R // 2 :, :R], c)
        total = part if total is None else total + part
    half_ref[...] = total


def last_levels(where_ref, own_ref, other_ref, *refs):
    @pl.when(where_ref[0] == 0)
    def _():
        last_body(where_ref, own_ref, other_ref, *refs)

    @pl.when(where_ref[0] == 1)
    def _():
        last_body(where_ref, other_ref, own_ref, *refs)


def last_body(where_ref, v1_ref, v2_ref, y_ref, out_ref, c_ref, d_ref, p_ref, z_ref):
    node = where_ref[2]
    pairs = ((node, node ^ 1), (node ^ 2, node ^ 3))
    systems = []
    for index, (a, b) in enumerate(pairs):
        product = dot(v1_ref[b, :, :R], v1_ref[a])
        right = v1_ref[b, :, R:] - product[:, R:]
        systems.append((product[:, :R], right, c_ref.at[index], p_ref.at[index]))
    solve(systems)
    sums = []
    for index, (a, b) in enumerate(pairs):
        coef_a = c_ref[index]
        coef_b = v1_ref[a, :, R:] - dot(v1_ref[a, :, :R], coef_a)
        total = None
        for place, c in ((a, coef_a), (b, coef_b)):
            part = v2_ref[place, :, R:] - dot(v2_ref[place, :, :R], c)
            total = part if total is None else total + part
        sums.append(total)
    own, other = sums
    z_ref[...] = y_ref[:, R:] - dot(y_ref[:, :R], c_ref[0])
    product = dot(other[:, :R], own)
    solve([(product[:, :R], other[:, R:] - product[:, R:], d_ref, p_ref.at[0])], rounds=3)
    out_ref[...] = (z_ref[:, R:] - dot(z_ref[:, :R], d_ref[...])).astype(BF16)


def lift_kernel(coef_ref, y_ref, out_ref):
    out_ref[...] = y_ref[:, R:] - dot(y_ref[:, :R], coef_ref[...])


def whole(kernel, outs, scratch, operands):
    smem = pl.BlockSpec(memory_space=pltpu.SMEM)
    vmem = pl.BlockSpec(memory_space=pltpu.VMEM)
    return pl.pallas_call(
        kernel,
        in_specs=[smem if x.ndim == 1 else vmem for x in operands],
        out_specs=[vmem] * len(outs) if len(outs) > 1 else vmem,
        out_shape=outs if len(outs) > 1 else outs[0],
        scratch_shapes=scratch,
        cost_estimate=pl.CostEstimate(flops=10**9, bytes_accessed=10**7, transcendentals=0),
        compiler_params=pltpu.CompilerParams(vmem_limit_bytes=VMEM_BYTES),
    )(*operands)


def local(coupling, rhs, left_factors, right_factors):
    leaves, rows = lax.axis_size("leaf"), lax.axis_size("row")
    leaf, row = lax.axis_index("leaf"), lax.axis_index("row")
    core, high, ring = row % 2, row // 2, rows // 2
    behind = (high + 2 * core - 1) % ring * 2
    ahead = (high - 2 * core + 1) % ring * 2
    far = (high + 2) % ring * 2
    where = [core, leaf % 2, leaf // 2 % 4, row, row ^ 1]
    where += [behind + core, behind + 1 - core, ahead + 1 - core, ahead + core, far + core, far + 1 - core]
    where = jnp.stack(where).astype(jnp.int32)
    swap = [(i, i ^ 1) for i in range(rows)]
    onward = [(i, (i + 2 - 4 * (i % 2)) % rows) for i in range(rows)]

    def move(value, way):
        return lax.ppermute(value, "row", way)

    block, v = coupling[0], right_factors[0]
    own = jnp.concatenate([left_factors[0], rhs[0]], axis=1)
    width, half = own.shape[1], v.shape[1] // 2
    y_shape = jax.ShapeDtypeStruct((BLOCK, width), F32)
    g_shape = jax.ShapeDtypeStruct((half, width), F32)

    def more(rows, cols, before):
        return whole(functools.partial(more_kernel, rows), [y_shape], [], (where, block, *cols, before))

    near = move(own, onward)
    own_s = move(own, swap)
    y = whole(start_kernel, [y_shape], [], (where, block, own))
    y = more((4,), (own_s,), y)
    own_s, y = lax.optimization_barrier((own_s, y))
    next_near = move(own_s, onward)
    far = move(near, onward)
    y = more((5,), (near,), y)
    near, y = lax.optimization_barrier((near, y))
    near_s = move(near, swap)
    y = more((6,), (next_near,), y)
    next_near, y = lax.optimization_barrier((next_near, y))
    next_near_s = move(next_near, swap)
    far_s = move(far, swap)
    y = more((7, 9), (near_s, far), y)
    y, keep, send = whole(
        far_kernel,
        [y_shape, g_shape, g_shape],
        [pltpu.VMEM((2 * half, width), F32)],
        (where, block, next_near_s, far_s, y, v),
    )
    keep = keep + move(send, swap)
    quarter = half // 4
    same_core = [list(range(c, rows, 2)) for c in range(2)]
    pieces = lax.all_to_all(keep.reshape(4, quarter, width), "row", 0, 0, tiled=True, axis_index_groups=same_core)
    piece = jnp.sum(pieces, axis=0)
    sibling = lax.ppermute(piece, "leaf", [(i, i ^ 1) for i in range(leaves)])
    both = jnp.stack([piece, sibling])
    mine = lax.all_gather(both, "row", axis=1, tiled=True, axis_index_groups=same_core)
    mine = mine.reshape(2, half, width)
    chip = [[2 * i, 2 * i + 1] for i in range(rows // 2)]
    pair = lax.all_gather(mine[:, : R // 2], "row", axis=0, axis_index_groups=chip)
    coef, part = whole(
        first_level,
        [jax.ShapeDtypeStruct((R, 3 * R), F32), jax.ShapeDtypeStruct((R, 3 * R), F32)],
        [pltpu.VMEM((R, R), F32)],
        (mine, pair),
    )
    window = [[8 * g + 2 * n + low for n in range(4)] for g in range(leaves // 8) for low in range(2)]
    nodes = lax.all_gather(part, "leaf", axis=0, axis_index_groups=window)
    others = move(nodes, swap)
    y = whole(lift_kernel, [jax.ShapeDtypeStruct((BLOCK, width - R), F32)], [], (coef, y))
    out = whole(
        last_levels,
        [jax.ShapeDtypeStruct((y.shape[0], R), BF16)],
        [
            pltpu.VMEM((2, R, 2 * R), F32),
            pltpu.VMEM((R, R), F32),
            pltpu.VMEM((2, R, R), F32),
            pltpu.VMEM((BLOCK, 2 * R), F32),
        ],
        (where, nodes, others, y),
    )
    return out[None]


def solution(mesh):
    spec = P("leaf", "row", None)
    return jax.shard_map(local, mesh=mesh, in_specs=(spec,) * 4, out_specs=spec, check_vma=False)
```

```python
import functools

import jax
import jax.numpy as jnp
from jax import lax
from jax.experimental import pallas as pl
from jax.experimental.pallas import tpu as pltpu
from jax.sharding import PartitionSpec as P

R = 128
BLOCK = 512
F32 = jnp.float32
BF16 = jnp.bfloat16
VMEM_BYTES = 16 * 1024 * 1024


def dot(a, b):
    return jnp.dot(a, b, precision=lax.Precision.HIGHEST, preferred_element_type=F32)


def invert(s, right, c_ref, p_ref):
    eye = (lax.broadcasted_iota(jnp.int32, (R, R), 0) == lax.broadcasted_iota(jnp.int32, (R, R), 1)).astype(F32)
    a = eye - s
    one = jnp.max(jnp.sum(jnp.abs(a), axis=0))
    most = jnp.max(jnp.sum(jnp.abs(a), axis=1))
    p_ref[...] = (a / one).T / most

    def again(state):
        step, old, new = state
        still = jnp.logical_or(new > 0.01, new < 0.25 * old)
        return jnp.logical_and(step < 200, jnp.logical_and(new > 1e-12, still))

    def newton(state):
        x = p_ref[...]
        res = eye - dot(a, x)
        p_ref[...] = x + dot(x, res)
        return (state[0] + 1, state[2], jnp.sum(res * res))

    lax.while_loop(again, newton, (jnp.int32(0), jnp.float32(1e30), jnp.float32(1e29)))
    x = p_ref[...]
    c_ref[...] = dot(x, right)
    for _ in range(2):
        c_ref[...] = c_ref[...] + dot(x, right - dot(a, c_ref[...]))


def solve(systems, rounds=2):
    left = jnp.zeros((R, R), F32)
    grown = jnp.zeros((R, R), F32)
    for s, right, c_ref, p_ref in systems:
        c = right + dot(s, right)
        p = dot(s, s)
        for _ in range(rounds):
            c = c + dot(p, c)
            p = dot(p, p)
        c_ref[...] = c
        p_ref[...] = p
        left = left + p * p
        grown = grown + s * s
    left = jnp.sum(left)
    good = jnp.logical_and(left < 0.25, jnp.sum(grown) < 64.0)

    @pl.when(good)
    def _():
        def more(_):
            size = jnp.zeros((R, R), F32)
            for _, _, c_ref, p_ref in systems:
                q = p_ref[...]
                c_ref[...] = c_ref[...] + dot(q, c_ref[...])
                q = dot(q, q)
                p_ref[...] = q
                size = size + q * q
            return jnp.sum(size)

        lax.while_loop(lambda size: size > 1e-13, more, left)

    @pl.when(jnp.logical_not(good))
    def _():
        for system in systems:
            invert(*system)


def column(row):
    return pl.ds(pl.multiple_of(row * BLOCK, BLOCK), BLOCK)


def terms(where_ref, block_ref, rows, cols_refs):
    blocks = jnp.concatenate([block_ref[:, column(where_ref[row])] for row in rows], axis=1)
    cols = jnp.concatenate([cols_ref[...] for cols_ref in cols_refs], axis=0)
    return jnp.dot(blocks, cols, preferred_element_type=F32)


def start_kernel(where_ref, block_ref, own_ref, y_ref):
    y_ref[...] = own_ref[...].astype(F32) + terms(where_ref, block_ref, (3,), (own_ref,))


def more_kernel(rows, where_ref, block_ref, *refs):
    *cols_refs, before_ref, y_ref = refs
    y_ref[...] = before_ref[...] + terms(where_ref, block_ref, rows, cols_refs)


def far_kernel(where_ref, block_ref, next_near_ref, far_ref, before_ref, v_ref, y_ref, keep_ref, send_ref, gram_ref):
    core = where_ref[0]
    y_ref[...] = before_ref[...] + terms(where_ref, block_ref, (8, 10), (next_near_ref, far_ref))
    rest = y_ref[...]
    total = None
    for _ in range(2):
        piece = rest.astype(BF16)
        rest = rest - piece.astype(F32)
        part = lax.dot_general(v_ref[...], piece, (((0,), (0,)), ((), ())), preferred_element_type=F32)
        total = part if total is None else total + part
    gram_ref[...] = total
    for part_ref, c in ((keep_ref, core), (send_ref, 1 - core)):
        part_ref[: R // 2, :] = gram_ref[pl.ds(pl.multiple_of(c * (R // 2), R // 2), R // 2), :]
        part_ref[R // 2 :, :] = gram_ref[pl.ds(pl.multiple_of(R + c * R, R), R), :]


def first_level(own_ref, pair_ref, coef_ref, half_ref, p_ref):
    lead, sibling = (jnp.concatenate([pair_ref[0, node], pair_ref[1, node]], axis=0) for node in range(2))
    product = dot(sibling[:, :R], lead)
    solve([(product[:, :R], sibling[:, R:] - product[:, R:], coef_ref, p_ref)])
    coef = coef_ref[...]
    coef_b = lead[:, R:] - dot(lead[:, :R], coef)
    total = None
    for node, c in ((0, coef), (1, coef_b)):
        part = own_ref[node, R // 2 :, R:] - dot(own_ref[node, R // 2 :, :R], c)
        total = part if total is None else total + part
    half_ref[...] = total


def last_levels(where_ref, own_ref, other_ref, *refs):
    @pl.when(where_ref[0] == 0)
    def _():
        last_body(where_ref, own_ref, other_ref, *refs)

    @pl.when(where_ref[0] == 1)
    def _():
        last_body(where_ref, other_ref, own_ref, *refs)


def last_body(where_ref, v1_ref, v2_ref, y_ref, out_ref, c_ref, d_ref, p_ref, z_ref):
    node = where_ref[2]
    pairs = ((node, node ^ 1), (node ^ 2, node ^ 3))
    systems = []
    for index, (a, b) in enumerate(pairs):
        product = dot(v1_ref[b, :, :R], v1_ref[a])
        right = v1_ref[b, :, R:] - product[:, R:]
        systems.append((product[:, :R], right, c_ref.at[index], p_ref.at[index]))
    solve(systems)
    sums = []
    for index, (a, b) in enumerate(pairs):
        coef_a = c_ref[index]
        coef_b = v1_ref[a, :, R:] - dot(v1_ref[a, :, :R], coef_a)
        total = None
        for place, c in ((a, coef_a), (b, coef_b)):
            part = v2_ref[place, :, R:] - dot(v2_ref[place, :, :R], c)
            total = part if total is None else total + part
        sums.append(total)
    own, other = sums
    z_ref[...] = y_ref[:, R:] - dot(y_ref[:, :R], c_ref[0])
    product = dot(other[:, :R], own)
    solve([(product[:, :R], other[:, R:] - product[:, R:], d_ref, p_ref.at[0])], rounds=3)
    out_ref[...] = (z_ref[:, R:] - dot(z_ref[:, :R], d_ref[...])).astype(BF16)


def lift_kernel(coef_ref, y_ref, out_ref):
    out_ref[...] = y_ref[:, R:] - dot(y_ref[:, :R], coef_ref[...])


def whole(kernel, outs, scratch, operands):
    smem = pl.BlockSpec(memory_space=pltpu.SMEM)
    vmem = pl.BlockSpec(memory_space=pltpu.VMEM)
    return pl.pallas_call(
        kernel,
        in_specs=[smem if x.ndim == 1 else vmem for x in operands],
        out_specs=[vmem] * len(outs) if len(outs) > 1 else vmem,
        out_shape=outs if len(outs) > 1 else outs[0],
        scratch_shapes=scratch,
        cost_estimate=pl.CostEstimate(flops=10**9, bytes_accessed=10**7, transcendentals=0),
        compiler_params=pltpu.CompilerParams(vmem_limit_bytes=VMEM_BYTES),
    )(*operands)


def local(coupling, rhs, left_factors, right_factors):
    leaves, rows = lax.axis_size("leaf"), lax.axis_size("row")
    leaf, row = lax.axis_index("leaf"), lax.axis_index("row")
    core, high, ring = row % 2, row // 2, rows // 2
    behind = (high + 2 * core - 1) % ring * 2
    ahead = (high - 2 * core + 1) % ring * 2
    far = (high + 2) % ring * 2
    where = [core, leaf % 2, leaf // 2 % 4, row, row ^ 1]
    where += [behind + core, behind + 1 - core, ahead + 1 - core, ahead + core, far + core, far + 1 - core]
    where = jnp.stack(where).astype(jnp.int32)
    swap = [(i, i ^ 1) for i in range(rows)]
    onward = [(i, (i + 2 - 4 * (i % 2)) % rows) for i in range(rows)]

    def move(value, way):
        return lax.ppermute(value, "row", way)

    block, v = coupling[0], right_factors[0]
    own = jnp.concatenate([left_factors[0], rhs[0]], axis=1)
    width, half = own.shape[1], v.shape[1] // 2
    y_shape = jax.ShapeDtypeStruct((BLOCK, width), F32)
    g_shape = jax.ShapeDtypeStruct((half, width), F32)

    def more(rows, cols, before):
        return whole(functools.partial(more_kernel, rows), [y_shape], [], (where, block, *cols, before))

    near = move(own, onward)
    own_s = move(own, swap)
    y = whole(start_kernel, [y_shape], [], (where, block, own))
    y = more((4,), (own_s,), y)
    own_s, y = lax.optimization_barrier((own_s, y))
    next_near = move(own_s, onward)
    far = move(near, onward)
    y = more((5,), (near,), y)
    near, y = lax.optimization_barrier((near, y))
    near_s = move(near, swap)
    y = more((6,), (next_near,), y)
    next_near, y = lax.optimization_barrier((next_near, y))
    next_near_s = move(next_near, swap)
    far_s = move(far, swap)
    y = more((7, 9), (near_s, far), y)
    y, keep, send = whole(
        far_kernel,
        [y_shape, g_shape, g_shape],
        [pltpu.VMEM((2 * half, width), F32)],
        (where, block, next_near_s, far_s, y, v),
    )
    keep = keep + move(send, swap)
    quarter = half // 4
    same_core = [list(range(c, rows, 2)) for c in range(2)]
    pieces = lax.all_to_all(keep.reshape(4, quarter, width), "row", 0, 0, tiled=True, axis_index_groups=same_core)
    piece = jnp.sum(pieces, axis=0)
    sibling = lax.ppermute(piece, "leaf", [(i, i ^ 1) for i in range(leaves)])
    both = jnp.stack([piece, sibling])
    mine = lax.all_gather(both, "row", axis=1, tiled=True, axis_index_groups=same_core)
    mine = mine.reshape(2, half, width)
    chip = [[2 * i, 2 * i + 1] for i in range(rows // 2)]
    pair = lax.all_gather(mine[:, : R // 2], "row", axis=0, axis_index_groups=chip)
    coef, part = whole(
        first_level,
        [jax.ShapeDtypeStruct((R, 3 * R), F32), jax.ShapeDtypeStruct((R, 3 * R), F32)],
        [pltpu.VMEM((R, R), F32)],
        (mine, pair),
    )
    window = [[8 * g + 2 * n + low for n in range(4)] for g in range(leaves // 8) for low in range(2)]
    nodes = lax.all_gather(part, "leaf", axis=0, axis_index_groups=window)
    others = move(nodes, swap)
    y = whole(lift_kernel, [jax.ShapeDtypeStruct((BLOCK, width - R), F32)], [], (coef, y))
    out = whole(
        last_levels,
        [jax.ShapeDtypeStruct((y.shape[0], R), BF16)],
        [
            pltpu.VMEM((2, R, 2 * R), F32),
            pltpu.VMEM((R, R), F32),
            pltpu.VMEM((2, R, R), F32),
            pltpu.VMEM((BLOCK, 2 * R), F32),
        ],
        (where, nodes, others, y),
    )
    return out[None]


def solution(mesh):
    spec = P("leaf", "row", None)
    return jax.shard_map(local, mesh=mesh, in_specs=(spec,) * 4, out_specs=spec, check_vma=False)
```
